128 devices in a mesh: section: 2 (over core), kvp: 16 (over y, x), tp: 4 (over z).
Axes of the slice: x: 4, y: 4, z: 4, core: 2. Of those that a mesh axis runs over, the one named last changes fastest.
Arguments:
- tokens: bfloat16 [512, 8192], P(None, ('kvp', 'tp')), may hold values from -1.5 to 1.5
- norm_gain: bfloat16 [2, 8192], P('section', 'kvp'), may hold values from 0.25 to 1.75
- query_weight: bfloat16 [2, 8192, 8192], P('section', 'kvp', 'tp'), may hold values from -0.0625 to 0.0625
- kv_weight: bfloat16 [2, 2, 8192, 1024], P('section', None, 'kvp', 'tp'), may hold values from -0.125 to 0.125
- out_weight: bfloat16 [2, 8192, 8192], P('section', 'tp', 'kvp'), may hold values from -0.09375 to 0.09375
- cache: bfloat16 [2, 2, 16384, 1024], P('section', None, 'kvp', 'tp'), may hold values from -90 to 90
- lengths: int32 [16], P('kvp'), may hold values from 1 to 1024, 12288 in all
Outputs:
- hidden_states: bfloat16 [2, 512, 8192], P('section', None, ('kvp', 'tp'))
The draws below stay inside these ranges and needn't reach their ends.
All inputs are finite; a program needn't handle non-finite values. No bound on the sum of `lengths` on one device may be relied on, other than what follows from the above.
Results may differ from the reference program's by a relative error of at most 0.034.
Values may be sent and summed in bfloat16 or wider, within the bound.
A program may use at most 128 MiB of HBM per device.

```python
import math
import jax
import jax.numpy as jnp
import numpy as np
from jax import lax

D = 8192
HEADS = 64
KV_HEADS = 8
HEAD_DIM = 128
CACHE_DEV = 1024
LAYERS = 2
ROWS = 512
CACHE = 16384
N_KVP = 16


def draw_cache(key, part):
    key = jax.random.fold_in(key, 11)
    shape = (LAYERS, 2, CACHE, KV_HEADS * HEAD_DIM)
    key_half = jnp.arange(2).reshape(1, 2, 1, 1) == 0
    base = jnp.clip(jax.random.normal(key, shape, jnp.float32), -6.0, 6.0)
    return (base * jnp.where(key_half, 2.0, 1.0)).astype(jnp.bfloat16)


def block_levels(key, shape, cuts, smallest, largest):
    factor_of, own = 1.0, jax.random.fold_in(key, 6)
    for axis_at, shards_of in cuts:
        steps = jnp.exp(jax.random.uniform(jax.random.fold_in(own, axis_at), (shards_of,), jnp.float32, smallest / len(cuts), largest / len(cuts)))
        factor_of = factor_of * jnp.repeat(steps, shape[axis_at] // shards_of).reshape([-1 if axis == axis_at else 1 for axis in range(len(shape))])
    return factor_of


def length_profile(number_of, total, most, slope):
    loads = [(1 << 20) // math.isqrt(grade ** slope) + 1 for grade in range(2, number_of + 1)]
    spare, holding = total - most - (number_of - 1), [1] * (number_of - 1)
    while spare > 0:
        movable = [i for i in range(number_of - 1) if holding[i] < most]
        mass, budget = sum([loads[i] for i in movable]), spare
        for i in movable:
            more = min(most - holding[i], max(1, budget * loads[i] // mass), spare)
            holding[i] = holding[i] + more
            spare = spare - more
    return np.array([most] + holding)


def ragged(key, count, total, bound, skew):
    if count == 2:
        one = jax.random.randint(key, (), max(1, total - bound), min(bound, total - 1) + 1)
        return jnp.stack([one, total - one])
    sizes = jnp.asarray(length_profile(count, total, bound, skew), jnp.int32)
    twos = (count - 1) // 2
    giver, receiver = sizes[1:1 + 2 * twos:2], sizes[2:2 + 2 * twos:2]
    slack = jnp.minimum(giver - 1, bound - receiver)
    shifted = jax.random.randint(jax.random.fold_in(key, 1), (twos,), 0, 1 << 20) % (slack + 1)
    sizes = sizes.at[1:1 + 2 * twos:2].set(giver - shifted).at[2:2 + 2 * twos:2].set(receiver + shifted)
    return sizes[jax.random.permutation(jax.random.fold_in(key, 2), count)]


def bell_draw(key, dims, width, most, cuts=(), dtype=jnp.bfloat16):
    gain = block_levels(key, dims, cuts, -0.22, 0.18) if cuts else 1.0
    drawn = jax.random.normal(key, dims, jnp.float32) * width * gain
    return jnp.minimum(jnp.maximum(drawn, -most), most).astype(dtype)


def setup_inputs(seed: int = 0) -> dict:
    key_list = jax.random.split(jax.random.key(seed), 8)
    return {
        "tokens": bell_draw(key_list[0], (ROWS, D), 0.25, 1.5, ((1, 64),)),
        "norm_gain": jnp.clip(1.0 + 0.15 * jax.random.normal(key_list[1], (LAYERS, D), jnp.float32), 0.25, 1.75).astype(jnp.bfloat16),
        "query_weight": bell_draw(key_list[2], (LAYERS, D, HEADS * HEAD_DIM), D ** -0.5, 0.0625, ((0, 2), (1, 16), (2, 4))),
        "kv_weight": bell_draw(key_list[3], (LAYERS, 2, D, KV_HEADS * HEAD_DIM), (D // 4) ** -0.5, 0.125, ((0, 2), (2, 16), (3, 4))),
        "out_weight": bell_draw(key_list[4], (LAYERS, HEADS * HEAD_DIM, D), (HEADS * HEAD_DIM // 2) ** -0.5, 0.09375, ((0, 2), (1, 4), (2, 16))),
        "cache": draw_cache(jax.random.fold_in(key_list[7], 71), 0),
        "lengths": ragged(key_list[6], N_KVP, N_KVP * CACHE_DEV * 3 // 4, CACHE_DEV, 0).astype(jnp.int32),
    }


def reference(tokens, norm_gain, query_weight, kv_weight, out_weight, cache, lengths):
    rows = tokens.shape[0]
    group = HEADS // KV_HEADS
    slots = jnp.arange(CACHE)
    owner = slots // CACHE_DEV
    live = (slots % CACHE_DEV < lengths[owner]).reshape(N_KVP, CACHE_DEV)
    positions = jnp.arange(rows)
    causal = positions[None, :] <= positions[:, None]
    inv_root = 1.0 / HEAD_DIM ** 0.5
    hidden = tokens
    collected = []
    for layer in range(LAYERS):
        base = hidden.astype(jnp.float32)
        factor = lax.rsqrt(lax.optimization_barrier(jnp.sum(base * base, axis=1)) / D + 1e-05)
        scaled = (base * norm_gain[layer].astype(jnp.float32)).astype(jnp.bfloat16)
        queries = (jnp.dot(scaled, query_weight[layer], preferred_element_type=jnp.float32) * factor[:, None]).astype(jnp.bfloat16)
        new_keys = (jnp.dot(scaled, kv_weight[layer, 0], preferred_element_type=jnp.float32) * factor[:, None]).astype(jnp.bfloat16)
        new_values = (jnp.dot(scaled, kv_weight[layer, 1], preferred_element_type=jnp.float32) * factor[:, None]).astype(jnp.bfloat16)
        grouped = queries.astype(jnp.float32).reshape(rows, KV_HEADS, group, HEAD_DIM)
        old_keys = cache[layer, 0].astype(jnp.float32).reshape(N_KVP, CACHE_DEV, KV_HEADS, HEAD_DIM)
        old_values = cache[layer, 1].astype(jnp.float32).reshape(N_KVP, CACHE_DEV, KV_HEADS, HEAD_DIM)
        fresh_keys = new_keys.astype(jnp.float32).reshape(rows, KV_HEADS, HEAD_DIM)
        fresh_values = new_values.astype(jnp.float32).reshape(rows, KV_HEADS, HEAD_DIM)
        cache_scores = jnp.einsum('rkgd,bckd->rkgbc', grouped, old_keys) * inv_root
        cache_scores = jnp.where(live[None, None, None, :, :], cache_scores, -jnp.inf)
        new_scores = jnp.einsum('rkgd,ckd->rkgc', grouped, fresh_keys) * inv_root
        new_scores = jnp.where(causal[:, None, None, :], new_scores, -jnp.inf)
        peaks = lax.optimization_barrier(jnp.max(cache_scores, axis=4))
        first_peak = jnp.maximum(peaks[..., 0], lax.optimization_barrier(jnp.max(new_scores, axis=3)))
        peaks = peaks.at[..., 0].set(first_peak)
        cache_weights = jnp.exp(cache_scores - peaks[..., None])
        new_weights = jnp.exp(new_scores - first_peak[..., None])
        totals = lax.optimization_barrier(jnp.sum(cache_weights, axis=4))
        totals = totals.at[..., 0].add(lax.optimization_barrier(jnp.sum(new_weights, axis=3)))
        cache_rounded = lax.optimization_barrier(cache_weights.astype(jnp.bfloat16)).astype(jnp.float32)
        new_rounded = lax.optimization_barrier(new_weights.astype(jnp.bfloat16)).astype(jnp.float32)
        parts = jnp.einsum('rkgbc,bckd->rkgbd', cache_rounded, old_values)
        parts = parts.at[:, :, :, 0, :].add(jnp.einsum('rkgc,ckd->rkgd', new_rounded, fresh_values))
        top = lax.optimization_barrier(jnp.max(peaks, axis=3))
        scale_by = jnp.exp(peaks - top[..., None])
        weight_sum = lax.optimization_barrier(jnp.sum(scale_by * totals, axis=3))
        merged = lax.optimization_barrier(jnp.sum(scale_by[..., None] * parts, axis=3))
        attended = (merged / weight_sum[..., None]).astype(jnp.bfloat16).reshape(rows, HEADS * HEAD_DIM)
        update = jnp.dot(attended, out_weight[layer], preferred_element_type=jnp.float32)
        hidden = (base + update).astype(jnp.bfloat16)
        collected.append(hidden)
    return jnp.stack(collected)
```

```python
import functools
import math

import jax
import jax.numpy as jnp
from jax import lax
from jax.experimental import pallas as pl
from jax.experimental.pallas import tpu as pltpu
from jax.sharding import PartitionSpec as P

LAYERS = 2
ROWS = 512
HALF = 256
GROUP = 128
D = 8192
FEAT = 512
HEAD = 128
PAIR = 256
SLOTS = 1024
EXP_SCALE = math.log2(math.e) / math.sqrt(HEAD)
BF = jnp.bfloat16
F32 = jnp.float32
FAR_FIRST = (2, 1, 3)


def mod4(value):
    return lax.rem(value, 4)


def dot(left, right):
    return jnp.dot(left, right, preferred_element_type=F32)


def dot_t(left, right):
    return lax.dot_general(left, right, (((1,), (1,)), ((), ())), preferred_element_type=F32)


def kernel(
    tok, gain, wq_in, wkv_in, wo_in, cache_in, len_in, out,
    wq, wkv, wo, kvc, hid, scaled, gains, lens, pq, rq, pkv, rkv, sq, fac,
    c2, r2, c2kv, r2kv, qry, newkv, peak, total, acc, stat, racc, rstat, att,
    mix, rmix, zs, zr, fin, ssem, rsem, wsem, wssem, csem, cssem,
):
    s = lax.axis_index("section")
    k = lax.axis_index("kvp")
    t = lax.axis_index("tp")
    y = k // 4
    x = lax.rem(k, 4)
    a = (1 - s) * x + s * y
    b = (1 - s) * y + s * x
    other = 1 - s

    def chip(i, j):
        return i * (1 + 3 * s) + j * (4 - 3 * s)

    def along_a(d):
        return {"kvp": chip(mod4(a + d), b)}

    def along_b(d):
        return {"kvp": chip(a, mod4(b + d))}

    def rows(start, size):
        return pl.ds(pl.multiple_of(start, 16), size)

    def cols(start, size):
        return pl.ds(pl.multiple_of(start, 128), size)

    used = [0]
    started = []

    def send(src, dst, dev):
        i = used[0]
        used[0] += 1
        c = pltpu.make_async_remote_copy(
            src_ref=src, dst_ref=dst, send_sem=ssem.at[i], recv_sem=rsem.at[i],
            device_id=dev, device_id_type=pl.DeviceIdType.MESH,
        )
        c.start()
        started.append(c)
        return c

    def weight_parts(h):
        return [
            (wq_in.at[0, :, cols(h * 1024, 1024)], wq.at[s]),
            (wkv_in.at[0, 0, :, cols(h * HEAD, HEAD)], wkv.at[s, :, pl.ds(0, HEAD)]),
            (wkv_in.at[0, 1, :, cols(h * HEAD, HEAD)], wkv.at[s, :, pl.ds(HEAD, HEAD)]),
            (wo_in.at[0, rows(h * 1024, 1024), :], wo.at[s]),
        ]

    def weights_local():
        return [
            pltpu.make_async_copy(src, dst, wsem.at[s * 5 + i])
            for i, (src, dst) in enumerate(weight_parts(s))
        ]

    def weights_remote():
        parts = weight_parts(other) + [(gains.at[s], gains.at[s])]
        return [
            pltpu.make_async_remote_copy(
                src_ref=src, dst_ref=dst, send_sem=wssem.at[i], recv_sem=wsem.at[s * 5 + i],
                device_id={"section": other}, device_id_type=pl.DeviceIdType.MESH,
            )
            for i, (src, dst) in enumerate(parts)
        ]

    def weight_wait(l, i):
        dst = (wq.at[l], wkv.at[l, :, pl.ds(0, HEAD)], wkv.at[l, :, pl.ds(HEAD, HEAD)], wo.at[l])[i]
        pltpu.make_async_copy(dst, dst, wsem.at[l * 5 + i]).wait()

    def cache_local():
        return pltpu.make_async_copy(
            cache_in.at[0, :, :, cols(s * HEAD, HEAD)],
            kvc.at[s, :, rows(a * SLOTS, SLOTS), :],
            csem.at[s * 4],
        )

    def cache_remote():
        made = []

        def add(head, place, d, dev):
            made.append(
                pltpu.make_async_remote_copy(
                    src_ref=cache_in.at[0, :, :, cols(head * HEAD, HEAD)],
                    dst_ref=kvc.at[s, :, rows(place * SLOTS, SLOTS), :],
                    send_sem=cssem.at[len(made)], recv_sem=csem.at[s * 4 + d],
                    device_id=dev, device_id_type=pl.DeviceIdType.MESH,
                )
            )

        add(other, b, 0, {"section": other})
        for d in FAR_FIRST:
            add(s, a, d, along_a(d))
            add(other, b, d, {"section": other, **along_b(d)})
        return made

    def cache_wait(l, d):
        dst = kvc.at[l, :, rows(mod4(a + 4 - d) * SLOTS, SLOTS), :]
        pltpu.make_async_copy(dst, dst, csem.at[l * 4 + d]).wait()

    local = weights_local()
    for c in local:
        c.start()
    here = cache_local()
    here.start()
    gains[s] = jnp.broadcast_to(gain[...].astype(F32), (8, FEAT))
    lens[a] = jnp.full((8, 128), len_in[0], jnp.int32)

    barrier = pltpu.get_barrier_semaphore()
    greeted = [{"kvp": lax.rem(k + d, 16)} for d in range(1, 16)]
    greeted += [{"tp": mod4(t + d)} for d in range(1, 4)]
    greeted += [{"section": other}]
    greeted += [{"section": other, **along_a(d)} for d in range(1, 4)]
    greeted += [{"section": other, **along_b(d)} for d in range(1, 4)]
    for dev in greeted:
        pl.semaphore_signal(barrier, inc=1, device_id=dev, device_id_type=pl.DeviceIdType.MESH)
    pl.semaphore_wait(barrier, len(greeted))

    def spread(l, src):
        def at(ref_rows, owner):
            return hid.at[l, rows(ref_rows * HALF, HALF), cols(owner * HEAD, HEAD)]

        moves = [(d, send(src, at(s, t), {"tp": mod4(t + d)})) for d in FAR_FIRST]
        swaps = [send(src, at(s, t), {"section": other})]
        return moves, swaps, at

    def spread_end(l, moves, swaps, at):
        for d, c in moves[1:] + moves[:1]:
            c.wait_recv()
            got = at(s, mod4(t + 4 - d))
            swaps.append(send(got, got, {"section": other}))
        for c in swaps:
            c.wait_recv()

    mine = tok.at[rows(s * HALF, HALF), :]
    pending = spread(0, mine)
    remote_w = weights_remote()
    for i in (0, 4, 1, 2, 3):
        remote_w[i].start()
    remote_c = cache_remote()

    @pl.when(s == 0)
    def _():
        for c in remote_c:
            c.start()

    len_moves = [send(lens.at[a], lens.at[a], along_a(d)) for d in FAR_FIRST]
    hid[0, rows(s * HALF, HALF), cols(t * HEAD, HEAD)] = tok[rows(s * HALF, HALF), :]

    lane = lax.broadcasted_iota(jnp.int32, (GROUP, 128), 1) % 4
    slot = lax.broadcasted_iota(jnp.int32, (1, SLOTS), 1)

    def block_step(q2, keys, values, bias, at):
        scores = dot_t(q2, keys) + bias
        top = jnp.max(scores, axis=1, keepdims=True)
        weights = jnp.exp2((scores - top) * EXP_SCALE)
        summed = jnp.sum(weights, axis=1, keepdims=True)
        part = dot(weights.astype(BF), values)
        old = peak[at]
        new = jnp.maximum(old, top)
        keep = jnp.exp2((old - new) * EXP_SCALE)
        add = jnp.exp2((top - new) * EXP_SCALE)
        peak[at] = new
        total[at] = total[at] * keep + summed * add
        return keep, add, part

    for l in range(LAYERS):
        spread_end(l, *pending)

        @pl.when(s != l)
        def _(l=l):
            pltpu.make_async_copy(gains.at[l], gains.at[l], wsem.at[l * 5 + 4]).wait()

        wide = hid[l].astype(F32)
        squares = wide * wide
        folded = squares[:, 0:128] + squares[:, 128:256] + squares[:, 256:384] + squares[:, 384:512]
        sq[l, 0] = jnp.sum(folded.T, axis=0, keepdims=True)
        sq_moves = [
            send(sq.at[l, 0], sq.at[l, d], {"kvp": lax.rem(k + d, 16)}) for d in range(1, 16)
        ]
        scaled[...] = (wide * gains[l, 0:1, :]).astype(BF)
        weight_wait(l, 0)

        first = {}
        for g in FAR_FIRST + (0,):
            span = rows(mod4(b + g) * GROUP, GROUP)
            for d in FAR_FIRST + (0,):
                head_cols = cols(mod4(a + d) * PAIR, PAIR)
                pq[l, d, span, :] = dot(scaled[span, :], wq[l, :, head_cols])
                if d:
                    first[g, d] = send(pq.at[l, d, span, :], rq.at[l, d - 1, span, :], along_a(d))
        weight_wait(l, 1)
        weight_wait(l, 2)
        pkv[l] = dot(scaled[...], wkv[l])
        first_kv = {
            d: send(pkv.at[l, rows(mod4(a + d) * GROUP, GROUP), :], rkv.at[l, d - 1], along_a(d))
            for d in FAR_FIRST
        }

        for c in sq_moves:
            c.wait_recv()
        square_sum = sq[l, 0]
        for d in range(1, 16):
            square_sum = square_sum + sq[l, d]
        factor = lax.rsqrt(square_sum / D + 1e-05)
        fac[...] = jnp.broadcast_to(factor, (128, ROWS)).T

        second = {}
        for g in FAR_FIRST + (0,):
            span = rows(mod4(b + g) * GROUP, GROUP)
            for d in FAR_FIRST:
                first[g, d].wait_recv()
            c2[l, span, :] = (pq[l, 0, span, :] + rq[l, 0, span, :]) + (
                rq[l, 1, span, :] + rq[l, 2, span, :]
            )
            if g:
                second[g] = send(c2.at[l, span, :], r2.at[l, g - 1], along_b(g))
        own = rows(b * GROUP, GROUP)
        for g in FAR_FIRST:
            second[g].wait_recv()
        q_sum = (c2[l, own, :] + r2[l, 0]) + (r2[l, 1] + r2[l, 2])
        own_fac = fac[own, :]
        q_fac = jnp.concatenate([own_fac, own_fac], axis=1)
        qry[l, own, :] = (q_sum * q_fac).astype(BF)
        q_moves = {d: send(qry.at[l, own, :], qry.at[l, own, :], along_b(d)) for d in FAR_FIRST}

        for d in FAR_FIRST:
            first_kv[d].wait_recv()
        c2kv[l] = (pkv[l, rows(a * GROUP, GROUP), :] + rkv[l, 0]) + (rkv[l, 1] + rkv[l, 2])
        second_kv = [
            send(c2kv.at[l, rows(mod4(b + d) * 32, 32), :], r2kv.at[l, d - 1], along_b(d))
            for d in FAR_FIRST
        ]
        for c in second_kv:
            c.wait_recv()
        kv_sum = (c2kv[l, rows(b * 32, 32), :] + r2kv[l, 0]) + (r2kv[l, 1] + r2kv[l, 2])
        kv_rows = rows(a * GROUP + b * 32, 32)
        kv_fac = fac[kv_rows, :]
        newkv[l, kv_rows, :] = (kv_sum * jnp.concatenate([kv_fac, kv_fac], axis=1)).astype(BF)
        kv_moves = [
            send(newkv.at[l, kv_rows, :], newkv.at[l, kv_rows, :], {"kvp": lax.rem(k + d, 16)})
            for d in range(1, 16)
        ]

        if l == 0:
            for c in len_moves:
                c.wait_recv()
        for d in range(4):
            cache_wait(l, d)
        back = {}
        stats_back = {}
        for d in (0, 2, 1, 3):
            span = rows(mod4(b + 4 - d) * GROUP, GROUP)
            if d:
                q_moves[d].wait_recv()
            q2 = jnp.concatenate([qry[l, span, 0:HEAD], qry[l, span, HEAD:PAIR]], axis=0)
            peak[d] = jnp.full((PAIR, 128), -jnp.inf, F32)
            total[d] = jnp.zeros((PAIR, 128), F32)
            acc[l, d] = jnp.zeros((PAIR, 128), F32)

            def one_block(c, carry, d=d, q2=q2, l=l):
                place = rows(c * SLOTS, SLOTS)
                bias = jnp.where(slot < lens[c, 0:1, 0:1], 0.0, -jnp.inf)
                keep, add, part = block_step(q2, kvc[l, 0, place, :], kvc[l, 1, place, :], bias, d)
                acc[l, d] = acc[l, d] * keep + part * add
                return carry

            lax.fori_loop(0, 4, one_block, 0)
            if d:
                stat[l, d] = jnp.where(
                    lane < 2,
                    jnp.where(lane == 0, peak[d, 0:GROUP, :], total[d, 0:GROUP, :]),
                    jnp.where(lane == 2, peak[d, GROUP:PAIR, :], total[d, GROUP:PAIR, :]),
                )
                back[d] = send(acc.at[l, d], racc.at[l, d - 1], along_b(4 - d))
                stats_back[d] = send(stat.at[l, d], rstat.at[l, d - 1], along_b(4 - d))

        if l == 0:
            @pl.when(s == 1)
            def _():
                for c in remote_c:
                    c.start()

        for c in kv_moves:
            c.wait_recv()
        q2 = jnp.concatenate([qry[l, own, 0:HEAD], qry[l, own, HEAD:PAIR]], axis=0)
        row_at = b * GROUP + lax.rem(lax.broadcasted_iota(jnp.int32, (PAIR, ROWS), 0), GROUP)
        key_at = lax.broadcasted_iota(jnp.int32, (PAIR, ROWS), 1)
        causal = jnp.where(key_at <= row_at, 0.0, -jnp.inf)
        keep, add, part = block_step(q2, newkv[l, :, 0:HEAD], newkv[l, :, HEAD:PAIR], causal, 0)
        acc[l, 0] = acc[l, 0] * keep + part * add

        for d in (2, 1, 3):
            back[d].wait_recv()
            stats_back[d].wait_recv()
        for j in range(2):
            part_rows = pl.ds(j * GROUP, GROUP)
            peaks = [peak[0, part_rows, :]]
            totals = [total[0, part_rows, :]]
            values = [acc[l, 0, part_rows, :]]
            for d in (1, 2, 3):
                st = rstat[l, d - 1]
                peaks.append(jnp.broadcast_to(st[:, 2 * j : 2 * j + 1], (GROUP, 128)))
                totals.append(jnp.broadcast_to(st[:, 2 * j + 1 : 2 * j + 2], (GROUP, 128)))
                values.append(racc[l, d - 1, part_rows, :])
            top = jnp.maximum(jnp.maximum(peaks[0], peaks[1]), jnp.maximum(peaks[2], peaks[3]))
            scale_by = [jnp.exp2((p - top) * EXP_SCALE) for p in peaks]
            weight_sum = sum(e * v for e, v in zip(scale_by, totals))
            merged = sum(e * v for e, v in zip(scale_by, values))
            att[l, a, own, pl.ds(j * HEAD, HEAD)] = (merged / weight_sum).astype(BF)

        spot = att.at[l, a, own, :]
        near = {d: send(spot, spot, along_b(d)) for d in FAR_FIRST}
        far = {(0, e): send(spot, spot, along_a(e)) for e in FAR_FIRST}
        for d in (1, 3, 2):
            near[d].wait_recv()
            got = att.at[l, a, rows(mod4(b + 4 - d) * GROUP, GROUP), :]
            for e in FAR_FIRST:
                far[d, e] = send(got, got, along_a(e))
        weight_wait(l, 3)
        mix[l] = dot(att[l, a], wo[l, rows(a * PAIR, PAIR), :])
        for e in (1, 3, 2):
            for d in (0, 1, 3, 2):
                far[d, e].wait_recv()
            source = mod4(a + 4 - e)
            mix[l] += dot(att[l, source], wo[l, rows(source * PAIR, PAIR), :])

        kept = rows(s * HALF, HALF)
        swap = send(mix.at[l, rows(other * HALF, HALF), :], rmix.at[l], {"section": other})
        swap.wait_recv()
        turns = {}
        for d in FAR_FIRST + (0,):
            block = cols(mod4(t + d) * HEAD, HEAD)
            zs[l, d] = mix[l, kept, block] + rmix[l, :, block]
            if d:
                turns[d] = send(zs.at[l, d], zr.at[l, d - 1], {"tp": mod4(t + d)})
        for d in FAR_FIRST:
            turns[d].wait_recv()
        mine_cols = cols(t * HEAD, HEAD)
        update = (zs[l, 0] + zr[l, 0]) + (zr[l, 1] + zr[l, 2])
        after = (hid[l, kept, mine_cols].astype(F32) + update).astype(BF)
        fin[l, kept, :] = after
        if l + 1 < LAYERS:
            hid[l + 1, kept, mine_cols] = after
            pending = spread(l + 1, fin.at[l, kept, :])
        else:
            last = send(fin.at[l, kept, :], fin.at[l, kept, :], {"section": other})
            last.wait_recv()

    out[...] = jnp.where(s == 0, hid[1, :, cols(t * HEAD, HEAD)], fin[1])
    for c in started:
        c.wait_send()
    for c in remote_w + remote_c:
        c.wait_send()


def per_device(tokens, norm_gain, query_weight, kv_weight, out_weight, cache, lengths):
    vmem = pl.BlockSpec(memory_space=pltpu.VMEM)
    anywhere = pl.BlockSpec(memory_space=pl.ANY)
    n = 200
    dma = pltpu.SemaphoreType.DMA
    scratch = [
        pltpu.VMEM((2, FEAT, 1024), BF),
        pltpu.VMEM((2, FEAT, PAIR), BF),
        pltpu.VMEM((2, 1024, FEAT), BF),
        pltpu.VMEM((2, 2, 4 * SLOTS, HEAD), BF),
        pltpu.VMEM((2, ROWS, FEAT), BF),
        pltpu.VMEM((ROWS, FEAT), BF),
        pltpu.VMEM((2, 8, FEAT), F32),
        pltpu.VMEM((4, 8, 128), jnp.int32),
        pltpu.VMEM((2, 4, ROWS, PAIR), F32),
        pltpu.VMEM((2, 3, ROWS, PAIR), F32),
        pltpu.VMEM((2, ROWS, PAIR), F32),
        pltpu.VMEM((2, 3, GROUP, PAIR), F32),
        pltpu.VMEM((2, 16, 1, ROWS), F32),
        pltpu.VMEM((ROWS, 128), F32),
        pltpu.VMEM((2, ROWS, PAIR), F32),
        pltpu.VMEM((2, 3, GROUP, PAIR), F32),
        pltpu.VMEM((2, GROUP, PAIR), F32),
        pltpu.VMEM((2, 3, 32, PAIR), F32),
        pltpu.VMEM((2, ROWS, PAIR), BF),
        pltpu.VMEM((2, ROWS, PAIR), BF),
        pltpu.VMEM((4, PAIR, 128), F32),
        pltpu.VMEM((4, PAIR, 128), F32),
        pltpu.VMEM((2, 4, PAIR, 128), F32),
        pltpu.VMEM((2, 4, GROUP, 128), F32),
        pltpu.VMEM((2, 3, PAIR, 128), F32),
        pltpu.VMEM((2, 3, GROUP, 128), F32),
        pltpu.VMEM((2, 4, ROWS, PAIR), BF),
        pltpu.VMEM((2, ROWS, FEAT), F32),
        pltpu.VMEM((2, HALF, FEAT), F32),
        pltpu.VMEM((2, 4, HALF, HEAD), F32),
        pltpu.VMEM((2, 3, HALF, HEAD), F32),
        pltpu.VMEM((2, ROWS, HEAD), BF),
        dma((n,)), dma((n,)), dma((10,)), dma((5,)), dma((8,)), dma((7,)),
    ]
    result = pl.pallas_call(
        kernel,
        out_shape=jax.ShapeDtypeStruct((ROWS, HEAD), BF),
        in_specs=[vmem, vmem, anywhere, anywhere, anywhere, anywhere,
                  pl.BlockSpec(memory_space=pltpu.SMEM)],
        out_specs=vmem,
        scratch_shapes=scratch,
        compiler_params=pltpu.CompilerParams(
            collective_id=0, has_side_effects=True, vmem_limit_bytes=60 * 2**20
        ),
    )(tokens, norm_gain, query_weight, kv_weight, out_weight, cache, lengths)
    return result[None]


def solution(mesh):
    placed = (
        P(None, ("kvp", "tp")),
        P("section", "kvp"),
        P("section", "kvp", "tp"),
        P("section", None, "kvp", "tp"),
        P("section", "tp", "kvp"),
        P("section", None, "kvp", "tp"),
        P("kvp"),
    )
    return jax.shard_map(
        per_device,
        mesh=mesh,
        in_specs=placed,
        out_specs=P("section", None, ("kvp", "tp")),
        check_vma=False,
    )
```

```python
import functools
import math

import jax
import jax.numpy as jnp
from jax import lax
from jax.experimental import pallas as pl
from jax.experimental.pallas import tpu as pltpu
from jax.sharding import PartitionSpec as P

LAYERS = 2
ROWS = 512
HALF = 256
GROUP = 128
PIECE = 64
D = 8192
FEAT = 512
HEAD = 128
PAIR = 256
SLOTS = 1024
EXP_SCALE = math.log2(math.e) / math.sqrt(HEAD)
BF = jnp.bfloat16
F32 = jnp.float32
FAR_FIRST = (2, 1, 3)
LAG = 1.5


def mod4(value):
    return lax.rem(value, 4)


def dot(left, right):
    return jnp.dot(left, right, preferred_element_type=F32)


def dot_t(left, right):
    return lax.dot_general(left, right, (((1,), (1,)), ((), ())), preferred_element_type=F32)


def kernel(
    tok, gain, wq_in, wkv_in, wo_in, cache_in, len_in, out,
    wq, wkv, wo, kvc, hid, scaled, gains, lens, pq, rq, pkv, rkv, fac,
    c2, r2, c2kv, r2kv, qry, newkv, acc, racc, att,
    mix, rmix, zs, zr, fin, ssem, rsem, wsem, wssem, csem, cssem,
):
    s = lax.axis_index("section")
    k = lax.axis_index("kvp")
    t = lax.axis_index("tp")
    y = k // 4
    x = lax.rem(k, 4)
    a = (1 - s) * x + s * y
    b = (1 - s) * y + s * x
    other = 1 - s

    def chip(i, j):
        return i * (1 + 3 * s) + j * (4 - 3 * s)

    def along_a(d):
        return {"kvp": chip(mod4(a + d), b)}

    def along_b(d):
        return {"kvp": chip(a, mod4(b + d))}

    def rows(start, size):
        return pl.ds(pl.multiple_of(start, 16), size)

    def cols(start, size):
        return pl.ds(pl.multiple_of(start, 128), size)

    used = [0]
    started = []

    def send(src, dst, dev):
        i = used[0]
        used[0] += 1
        c = pltpu.make_async_remote_copy(
            src_ref=src, dst_ref=dst, send_sem=ssem.at[i], recv_sem=rsem.at[i],
            device_id=dev, device_id_type=pl.DeviceIdType.MESH,
        )
        c.start()
        started.append(c)
        return c

    def weight_parts(h):
        return [
            (wq_in.at[0, :, cols(h * 1024, 1024)], wq.at[s]),
            (wkv_in.at[0, 0, :, cols(h * HEAD, HEAD)], wkv.at[s, :, pl.ds(0, HEAD)]),
            (wkv_in.at[0, 1, :, cols(h * HEAD, HEAD)], wkv.at[s, :, pl.ds(HEAD, HEAD)]),
            (wo_in.at[0, rows(h * 1024, 1024), :], wo.at[s]),
        ]

    def weights_local():
        return [
            pltpu.make_async_copy(src, dst, wsem.at[s * 5 + i])
            for i, (src, dst) in enumerate(weight_parts(s))
        ]

    def weights_remote():
        parts = weight_parts(other) + [(gains.at[s], gains.at[s])]
        return [
            pltpu.make_async_remote_copy(
                src_ref=src, dst_ref=dst, send_sem=wssem.at[i], recv_sem=wsem.at[s * 5 + i],
                device_id={"section": other}, device_id_type=pl.DeviceIdType.MESH,
            )
            for i, (src, dst) in enumerate(parts)
        ]

    def weight_wait(l, i):
        dst = (wq.at[l], wkv.at[l, :, pl.ds(0, HEAD)], wkv.at[l, :, pl.ds(HEAD, HEAD)], wo.at[l])[i]
        pltpu.make_async_copy(dst, dst, wsem.at[l * 5 + i]).wait()

    def cache_local():
        return [
            pltpu.make_async_copy(
                cache_in.at[0, i, :, cols(s * HEAD, HEAD)],
                kvc.at[s, i, rows(a * SLOTS, SLOTS), :],
                csem.at[s * 8 + i],
            )
            for i in range(2)
        ]

    def cache_remote(i):
        made = []

        def add(head, place, d, dev):
            made.append(
                pltpu.make_async_remote_copy(
                    src_ref=cache_in.at[0, i, :, cols(head * HEAD, HEAD)],
                    dst_ref=kvc.at[s, i, rows(place * SLOTS, SLOTS), :],
                    send_sem=cssem.at[i * 7 + len(made)], recv_sem=csem.at[s * 8 + d * 2 + i],
                    device_id=dev, device_id_type=pl.DeviceIdType.MESH,
                )
            )

        add(other, b, 0, {"section": other})
        for d in FAR_FIRST:
            add(s, a, d, along_a(d))
            add(other, b, d, {"section": other, **along_b(d)})
        return made

    def cache_wait(l, d):
        for i in range(2):
            dst = kvc.at[l, i, rows(mod4(a + 4 - d) * SLOTS, SLOTS), :]
            pltpu.make_async_copy(dst, dst, csem.at[l * 8 + d * 2 + i]).wait()

    local = weights_local()
    for c in local:
        c.start()
    for c in cache_local():
        c.start()
    gains[s] = jnp.broadcast_to(gain[...].astype(F32), (8, FEAT))
    lens[a] = jnp.full((8, 128), len_in[0], jnp.int32)

    barrier = pltpu.get_barrier_semaphore()
    greeted = [{"kvp": lax.rem(k + d, 16)} for d in range(1, 16)]
    greeted += [{"tp": mod4(t + d)} for d in range(1, 4)]
    greeted += [{"section": other}]
    greeted += [{"section": other, "tp": mod4(t + d)} for d in range(1, 4)]
    greeted += [{"section": other, **along_a(d)} for d in range(1, 4)]
    greeted += [{"section": other, **along_b(d)} for d in range(1, 4)]
    for dev in greeted:
        pl.semaphore_signal(barrier, inc=1, device_id=dev, device_id_type=pl.DeviceIdType.MESH)
    pl.semaphore_wait(barrier, len(greeted))

    def spread(l, h, src):
        spot = hid.at[l, rows(h * HALF + s * GROUP, GROUP), cols(t * HEAD, HEAD)]
        pending[l, h] = [send(src, spot, {"section": other})]
        for d in FAR_FIRST:
            pending[l, h] += [
                send(src, spot, {"tp": mod4(t + d)}),
                send(src, spot, {"tp": mod4(t + d), "section": other}),
            ]

    def front(l, h):
        for c in pending[l, h]:
            c.wait_recv()
        if h == 0:

            @pl.when(s != l)
            def _():
                pltpu.make_async_copy(gains.at[l], gains.at[l], wsem.at[l * 5 + 4]).wait()

        half = pl.ds(h * HALF, HALF)
        wide = hid[l, half, :].astype(F32)
        squares = wide * wide
        folded = (squares[:, 0:128] + squares[:, 128:256]) + (squares[:, 256:384] + squares[:, 384:512])
        squares_row = jnp.broadcast_to(jnp.sum(folded.T, axis=0, keepdims=True), (8, HALF))
        scaled[h] = (wide * gains[l, 0:1, :]).astype(BF)
        if h == 0:
            weight_wait(l, 0)
        for d in FAR_FIRST + (0,):
            pq[l, h, d, 0:HALF, :] = dot(scaled[h], wq[l, :, cols(mod4(a + d) * PAIR, PAIR)])
            pq[l, h, d, HALF:, :] = squares_row
            if d:
                first[l, h, d] = send(pq.at[l, h, d], rq.at[l, h, d - 1], along_a(d))
        if h == 0:
            weight_wait(l, 1)
            weight_wait(l, 2)
        pkv[l, h] = dot(scaled[h], wkv[l])
        for d in FAR_FIRST:
            piece = pkv.at[l, h, rows(mod4(a + d) * PIECE, PIECE), :]
            first_kv[l, h, d] = send(piece, rkv.at[l, h, d - 1], along_a(d))

    def sum_a(l, h):
        for d in FAR_FIRST:
            first[l, h, d].wait_recv()

        def summed(span):
            return (pq[l, h, 0, span, :] + rq[l, h, 0, span, :]) + (
                rq[l, h, 1, span, :] + rq[l, h, 2, span, :]
            )

        squares = summed(pl.ds(HALF, 8))
        for g in FAR_FIRST + (0,):
            c2[l, h, g, 0:PIECE, :] = summed(rows(mod4(b + g) * PIECE, PIECE))
            c2[l, h, g, PIECE:, :] = squares
            if g:
                second[l, h, g] = send(c2.at[l, h, g], r2.at[l, h, g - 1], along_b(g))

    def kv_a(l, h):
        for d in FAR_FIRST:
            first_kv[l, h, d].wait_recv()
        c2kv[l, h] = (pkv[l, h, rows(a * PIECE, PIECE), :] + rkv[l, h, 0]) + (rkv[l, h, 1] + rkv[l, h, 2])
        for d in FAR_FIRST:
            piece = c2kv.at[l, h, rows(mod4(b + d) * 16, 16), :]
            second_kv[l, h, d] = send(piece, r2kv.at[l, h, d - 1], along_b(d))

    def sum_b(l, h):
        for g in FAR_FIRST:
            second[l, h, g].wait_recv()
        full = (c2[l, h, 0] + r2[l, h, 0]) + (r2[l, h, 1] + r2[l, h, 2])
        factor = lax.rsqrt(full[PIECE : PIECE + 1] / D + 1e-05)
        fac[h] = jnp.broadcast_to(factor, (128, HALF)).T
        own_fac = fac[h, rows(b * PIECE, PIECE), :]
        own = rows(h * HALF + b * PIECE, PIECE)
        qry[l, own, :] = (full[0:PIECE] * jnp.concatenate([own_fac, own_fac], axis=1)).astype(BF)
        for d in FAR_FIRST:
            q_moves[l, h, d] = send(qry.at[l, own, :], qry.at[l, own, :], along_b(d))

    def kv_b(l, h):
        for d in FAR_FIRST:
            second_kv[l, h, d].wait_recv()
        kv_sum = (c2kv[l, h, rows(b * 16, 16), :] + r2kv[l, h, 0]) + (r2kv[l, h, 1] + r2kv[l, h, 2])
        kv_fac = fac[h, rows(a * PIECE + b * 16, 16), :]
        kv_rows = rows(h * HALF + a * PIECE + b * 16, 16)
        newkv[l, kv_rows, :] = (kv_sum * jnp.concatenate([kv_fac, kv_fac], axis=1)).astype(BF)
        kv_at[l, h] = used[0]
        used[0] += 16
        copies = kv_copies(l, h)
        for c in copies[1:]:
            c.start()

        @pl.when(b != 0)
        def _():
            copies[0].start()

    def kv_copies(l, h):
        spot = newkv.at[l, rows(h * HALF + a * PIECE + b * 16, 16), :]
        return [
            pltpu.make_async_remote_copy(
                src_ref=spot, dst_ref=spot, send_sem=ssem.at[kv_at[l, h] + d],
                recv_sem=rsem.at[kv_at[l, h] + d * 4 + b], device_id={"kvp": chip(mod4(a + d), 0)},
                device_id_type=pl.DeviceIdType.MESH,
            )
            for d in range(4)
        ]

    def kv_wait(l, h):
        for d in range(4):
            for j in range(4):
                if d or j:
                    dst = newkv.at[l, rows(h * HALF + mod4(a + 4 - d) * PIECE + j * 16, 16), :]
                    pltpu.make_async_copy(dst, dst, rsem.at[kv_at[l, h] + d * 4 + j]).wait()

    def attend(l, h):
        if h == 0:
            for d in range(4):
                cache_wait(l, d)
            if l == 0:
                for c in len_moves:
                    c.wait_recv()
        for d in FAR_FIRST:
            q_moves[l, h, d].wait_recv()

        def run(joint):
            parts = []
            for d in range(4):
                span = rows(h * HALF + mod4(b + 4 - d) * PIECE, PIECE)
                parts += [qry[l, span, 0:HEAD], qry[l, span, HEAD:PAIR]]
            q2 = jnp.concatenate(parts, axis=0)
            tops, sums, sides = [], [], []
            for c in (1, 2, 3, 0):
                place = pl.ds(c * SLOTS, SLOTS)
                bias = jnp.where(slot < lens[c, 0:1, 0:1], 0.0, -jnp.inf)
                scores = [dot_t(q2, kvc[l, 0, place, :]) + bias]
                values = [kvc[l, 1, place, :]]
                if joint and c == 0:
                    keys = (h + 1) * HALF
                    row_at = lax.rem(lax.broadcasted_iota(jnp.int32, (GROUP, keys), 0), PIECE)
                    key_at = lax.broadcasted_iota(jnp.int32, (GROUP, keys), 1)
                    ahead = key_at - row_at
                    causal = jnp.concatenate(
                        [
                            jnp.where(ahead <= h * HALF + (-d % 4) * PIECE, 0.0, -jnp.inf)
                            for d in range(4)
                        ],
                        axis=0,
                    )
                    scores.append(dot_t(q2, newkv[l, 0:keys, 0:HEAD]) + causal)
                    values.append(newkv[l, 0:keys, HEAD:PAIR])
                top = functools.reduce(
                    jnp.maximum, [jnp.max(v, axis=1, keepdims=True) for v in scores]
                )
                weights = [jnp.exp2((v - top) * EXP_SCALE) for v in scores]
                tops.append(top)
                sums.append(sum(jnp.sum(v, axis=1, keepdims=True) for v in weights))
                sides.append(sum(dot(w.astype(BF), v) for w, v in zip(weights, values)))
            peak = functools.reduce(jnp.maximum, tops)
            scale_by = [jnp.exp2((v - peak) * EXP_SCALE) for v in tops]
            total = sum(e * v for e, v in zip(scale_by, sums))
            merged = sum(e * v for e, v in zip(scale_by, sides))
            for d in range(4):
                piece = slice(d * GROUP, (d + 1) * GROUP)
                acc[l, h, d, 0:GROUP, :] = merged[piece]
                acc[l, h, d, GROUP:, :] = jnp.where(lane == 0, peak[piece], total[piece]).T[0:8]

        @pl.when(b == 0)
        def _():
            kv_wait(l, h)
            run(True)

        @pl.when(b != 0)
        def _():
            run(False)

        for d in (2, 3, 1):
            back[l, h, d] = send(acc.at[l, h, d], racc.at[l, h, d - 1], along_b(4 - d))

    def combine(l, h):
        for d in FAR_FIRST:
            back[l, h, d].wait_recv()
        own = rows(h * HALF + b * PIECE, PIECE)
        blocks = [acc[l, h, 0]] + [racc[l, h, d] for d in range(3)]
        stats = [jnp.concatenate([v[GROUP:]] * 16, axis=0).T for v in blocks]
        peaks = [v[:, 0:1] for v in stats]
        top = functools.reduce(jnp.maximum, peaks)
        scale_by = [jnp.exp2((v - top) * EXP_SCALE) for v in peaks]
        weight_sum = sum(e * v[:, 1:2] for e, v in zip(scale_by, stats))
        merged = sum(e * v[0:GROUP] for e, v in zip(scale_by, blocks))
        attended = (merged / weight_sum).astype(BF)
        att[l, a, own, 0:HEAD] = attended[0:PIECE]
        att[l, a, own, HEAD:PAIR] = attended[PIECE:GROUP]
        spot = att.at[l, a, own, :]
        for d in FAR_FIRST:
            near[l, h, d] = send(spot, spot, along_b(d))
        for e in FAR_FIRST:
            far[l, h, 0, e] = send(spot, spot, along_a(e))

    def forward(l, h):
        for d in (1, 3, 2):
            near[l, h, d].wait_recv()
            got = att.at[l, a, rows(h * HALF + mod4(b + 4 - d) * PIECE, PIECE), :]
            for e in FAR_FIRST:
                far[l, h, d, e] = send(got, got, along_a(e))

    def project(l, h):
        half = pl.ds(h * HALF, HALF)
        if h == 0:
            weight_wait(l, 3)
        summed = dot(att[l, a, half, :], wo[l, rows(a * PAIR, PAIR), :])
        for e in (1, 3, 2):
            for d in (0, 1, 3, 2):
                far[l, h, d, e].wait_recv()
            source = mod4(a + 4 - e)
            summed += dot(att[l, source, half, :], wo[l, rows(source * PAIR, PAIR), :])
        mix[l, half, :] = summed
        swaps[l, h] = send(
            mix.at[l, rows(h * HALF + other * GROUP, GROUP), :], rmix.at[l, h], {"section": other}
        )

    def turn(l, h):
        swaps[l, h].wait_recv()
        kept = rows(h * HALF + s * GROUP, GROUP)
        for d in FAR_FIRST + (0,):
            block = cols(mod4(t + d) * HEAD, HEAD)
            zs[l, h, d] = mix[l, kept, block] + rmix[l, h, :, block]
            if d:
                turns[l, h, d] = send(zs.at[l, h, d], zr.at[l, h, d - 1], {"tp": mod4(t + d)})

    def settle(l, h):
        for d in FAR_FIRST:
            turns[l, h, d].wait_recv()
        kept = rows(h * HALF + s * GROUP, GROUP)
        mine_cols = cols(t * HEAD, HEAD)
        update = (zs[l, h, 0] + zr[l, h, 0]) + (zr[l, h, 1] + zr[l, h, 2])
        after = (hid[l, kept, mine_cols].astype(F32) + update).astype(BF)
        fin[l, kept, :] = after
        if l + 1 < LAYERS:
            hid[l + 1, kept, mine_cols] = after
            spread(l + 1, h, fin.at[l, kept, :])
        else:
            ends.append(send(fin.at[l, kept, :], fin.at[l, kept, :], {"section": other}))

    pending, first, first_kv, second, second_kv = {}, {}, {}, {}, {}
    q_moves, kv_at, back, near, far, swaps, turns = {}, {}, {}, {}, {}, {}, {}
    ends = []
    lane = lax.rem(lax.broadcasted_iota(jnp.int32, (GROUP, 128), 1), 2)
    slot = lax.broadcasted_iota(jnp.int32, (1, SLOTS), 1)

    for h in range(2):
        spread(0, h, tok.at[rows(h * HALF + s * GROUP, GROUP), :])
    remote_w = weights_remote()
    for i in (0, 4, 1, 2, 3):
        remote_w[i].start()
    remote_k, remote_v = cache_remote(0), cache_remote(1)
    remote_c = remote_k + remote_v

    @pl.when(s == 0)
    def _():
        for c in remote_k:
            c.start()

    len_moves = [send(lens.at[a], lens.at[a], along_a(d)) for d in FAR_FIRST]
    for h in range(2):
        kept = rows(h * HALF + s * GROUP, GROUP)
        hid[0, kept, cols(t * HEAD, HEAD)] = tok[kept, :]
    drained = [0]

    def drain(upto):
        for c in started[drained[0] : upto]:
            c.wait_send()
        drained[0] = max(drained[0], upto)

    steps = (front, sum_a, kv_a, sum_b, kv_b, attend, combine, forward, project, turn, settle)
    order = sorted((i + LAG * h, h, i) for h in range(2) for i in range(LAYERS * len(steps)))
    marks = {}
    for _, h, i in order:
        l, step = i // len(steps), steps[i % len(steps)]
        if step == sum_b and h == 0 and l > 0:
            drain(marks[0])
        if step == sum_a and h == 0:
            marks[l] = len(started)
        if step == turn and l == 0 and h == 0:

            @pl.when(s == 1)
            def _():
                for c in remote_c:
                    c.start()

        step(l, h)
        if step == front and l == 0 and h == 0:

            @pl.when(s == 0)
            def _():
                for c in remote_v:
                    c.start()

    for c in ends:
        c.wait_recv()
    out[...] = jnp.where(s == 0, hid[1, :, cols(t * HEAD, HEAD)], fin[1])
    drain(len(started))
    for c in remote_w + remote_c:
        c.wait_send()

    moved = [kv_copies(l, h) for l in range(LAYERS) for h in range(2)]
    for copies in moved:
        for c in copies[1:]:
            c.wait_send()

    @pl.when(b != 0)
    def _():
        for copies in moved:
            copies[0].wait_send()


def per_device(tokens, norm_gain, query_weight, kv_weight, out_weight, cache, lengths):
    vmem = pl.BlockSpec(memory_space=pltpu.VMEM)
    anywhere = pl.BlockSpec(memory_space=pl.ANY)
    n = 300
    dma = pltpu.SemaphoreType.DMA
    scratch = [
        pltpu.VMEM((2, FEAT, 1024), BF),
        pltpu.VMEM((2, FEAT, PAIR), BF),
        pltpu.VMEM((2, 1024, FEAT), BF),
        pltpu.VMEM((2, 2, 4 * SLOTS, HEAD), BF),
        pltpu.VMEM((2, ROWS, FEAT), BF),
        pltpu.VMEM((2, HALF, FEAT), BF),
        pltpu.VMEM((2, 8, FEAT), F32),
        pltpu.VMEM((4, 8, 128), jnp.int32),
        pltpu.VMEM((2, 2, 4, HALF + 8, PAIR), F32),
        pltpu.VMEM((2, 2, 3, HALF + 8, PAIR), F32),
        pltpu.VMEM((2, 2, HALF, PAIR), F32),
        pltpu.VMEM((2, 2, 3, PIECE, PAIR), F32),
        pltpu.VMEM((2, HALF, 128), F32),
        pltpu.VMEM((2, 2, 4, PIECE + 8, PAIR), F32),
        pltpu.VMEM((2, 2, 3, PIECE + 8, PAIR), F32),
        pltpu.VMEM((2, 2, PIECE, PAIR), F32),
        pltpu.VMEM((2, 2, 3, 16, PAIR), F32),
        pltpu.VMEM((2, ROWS, PAIR), BF),
        pltpu.VMEM((2, ROWS, PAIR), BF),
        pltpu.VMEM((2, 2, 4, GROUP + 8, 128), F32),
        pltpu.VMEM((2, 2, 3, GROUP + 8, 128), F32),
        pltpu.VMEM((2, 4, ROWS, PAIR), BF),
        pltpu.VMEM((2, ROWS, FEAT), F32),
        pltpu.VMEM((2, 2, GROUP, FEAT), F32),
        pltpu.VMEM((2, 2, 4, GROUP, HEAD), F32),
        pltpu.VMEM((2, 2, 3, GROUP, HEAD), F32),
        pltpu.VMEM((2, ROWS, HEAD), BF),
        dma((n,)), dma((n,)), dma((10,)), dma((5,)), dma((16,)), dma((14,)),
    ]
    result = pl.pallas_call(
        kernel,
        out_shape=jax.ShapeDtypeStruct((ROWS, HEAD), BF),
        in_specs=[vmem, vmem, anywhere, anywhere, anywhere, anywhere,
                  pl.BlockSpec(memory_space=pltpu.SMEM)],
        out_specs=vmem,
        scratch_shapes=scratch,
        compiler_params=pltpu.CompilerParams(
            collective_id=0, has_side_effects=True, vmem_limit_bytes=60 * 2**20
        ),
    )(tokens, norm_gain, query_weight, kv_weight, out_weight, cache, lengths)
    return result[None]


def solution(mesh):
    placed = (
        P(None, ("kvp", "tp")),
        P("section", "kvp"),
        P("section", "kvp", "tp"),
        P("section", None, "kvp", "tp"),
        P("section", "tp", "kvp"),
        P("section", None, "kvp", "tp"),
        P("kvp"),
    )
    return jax.shard_map(
        per_device,
        mesh=mesh,
        in_specs=placed,
        out_specs=P("section", None, ("kvp", "tp")),
        check_vma=False,
    )
```

```python
import functools
import math

import jax
import jax.numpy as jnp
from jax import lax
from jax.experimental import pallas as pl
from jax.experimental.pallas import tpu as pltpu
from jax.sharding import PartitionSpec as P

LAYERS = 2
ROWS = 512
HALF = 256
GROUP = 128
PIECE = 64
D = 8192
FEAT = 512
HEAD = 128
PAIR = 256
SLOTS = 1024
EXP_SCALE = math.log2(math.e) / math.sqrt(HEAD)
BF = jnp.bfloat16
F32 = jnp.float32
FAR_FIRST = (2, 1, 3)
STARTS = (0, 1, 1.1, 2, 2.1, 3, 4, 5, 6, 7, 8)
PERIOD = 9
LAG = 1.5


def mod4(value):
    return lax.rem(value, 4)


def dot(left, right):
    return jnp.dot(left, right, preferred_element_type=F32)


def dot_t(left, right):
    return lax.dot_general(left, right, (((1,), (1,)), ((), ())), preferred_element_type=F32)


def kernel(
    tok, gain, wq_in, wkv_in, wo_in, cache_in, len_in, out,
    wq, wkv, wo, kvc, hid, scaled, gains, lens, pq, rq, pkv, rkv, fac,
    c2, r2, c2kv, r2kv, qry, newkv, acc, racc, att,
    mix, rmix, zs, zr, fin, ssem, rsem, wsem, wssem, csem, cssem,
):
    s = lax.axis_index("section")
    k = lax.axis_index("kvp")
    t = lax.axis_index("tp")
    y = k // 4
    x = lax.rem(k, 4)
    a = (1 - s) * x + s * y
    b = (1 - s) * y + s * x
    other = 1 - s

    def chip(i, j):
        return i * (1 + 3 * s) + j * (4 - 3 * s)

    def along_a(d):
        return {"kvp": chip(mod4(a + d), b)}

    def along_b(d):
        return {"kvp": chip(a, mod4(b + d))}

    def rows(start, size):
        return pl.ds(pl.multiple_of(start, 16), size)

    def cols(start, size):
        return pl.ds(pl.multiple_of(start, 128), size)

    used = [0]
    started = []

    def send(src, dst, dev):
        i = used[0]
        used[0] += 1
        c = pltpu.make_async_remote_copy(
            src_ref=src, dst_ref=dst, send_sem=ssem.at[i], recv_sem=rsem.at[i],
            device_id=dev, device_id_type=pl.DeviceIdType.MESH,
        )
        c.start()
        started.append(c)
        return c

    def weight_parts(h):
        return [
            (wq_in.at[0, :, cols(h * 1024, 1024)], wq.at[s]),
            (wkv_in.at[0, 0, :, cols(h * HEAD, HEAD)], wkv.at[s, :, pl.ds(0, HEAD)]),
            (wkv_in.at[0, 1, :, cols(h * HEAD, HEAD)], wkv.at[s, :, pl.ds(HEAD, HEAD)]),
            (wo_in.at[0, rows(h * 1024, 1024), :], wo.at[s]),
        ]

    def weights_local():
        return [
            pltpu.make_async_copy(src, dst, wsem.at[s * 5 + i])
            for i, (src, dst) in enumerate(weight_parts(s))
        ]

    def weights_remote():
        parts = weight_parts(other) + [(gains.at[s], gains.at[s])]
        return [
            pltpu.make_async_remote_copy(
                src_ref=src, dst_ref=dst, send_sem=wssem.at[i], recv_sem=wsem.at[s * 5 + i],
                device_id={"section": other}, device_id_type=pl.DeviceIdType.MESH,
            )
            for i, (src, dst) in enumerate(parts)
        ]

    def weight_wait(l, i):
        dst = (wq.at[l], wkv.at[l, :, pl.ds(0, HEAD)], wkv.at[l, :, pl.ds(HEAD, HEAD)], wo.at[l])[i]
        pltpu.make_async_copy(dst, dst, wsem.at[l * 5 + i]).wait()

    def cache_local():
        return [
            pltpu.make_async_copy(
                cache_in.at[0, i, :, cols(s * HEAD, HEAD)],
                kvc.at[s, i, rows(a * SLOTS, SLOTS), :],
                csem.at[s * 8 + i],
            )
            for i in range(2)
        ]

    def cache_remote(i):
        made = []

        def add(head, place, d, dev):
            made.append(
                pltpu.make_async_remote_copy(
                    src_ref=cache_in.at[0, i, :, cols(head * HEAD, HEAD)],
                    dst_ref=kvc.at[s, i, rows(place * SLOTS, SLOTS), :],
                    send_sem=cssem.at[i * 7 + len(made)], recv_sem=csem.at[s * 8 + d * 2 + i],
                    device_id=dev, device_id_type=pl.DeviceIdType.MESH,
                )
            )

        add(other, b, 0, {"section": other})
        for d in FAR_FIRST:
            add(s, a, d, along_a(d))
            add(other, b, d, {"section": other, **along_b(d)})
        return made

    def cache_wait(l, d):
        for i in range(2):
            dst = kvc.at[l, i, rows(mod4(a + 4 - d) * SLOTS, SLOTS), :]
            pltpu.make_async_copy(dst, dst, csem.at[l * 8 + d * 2 + i]).wait()

    local = weights_local()
    for c in local:
        c.start()
    for c in cache_local():
        c.start()
    gains[s] = jnp.broadcast_to(gain[...].astype(F32), (8, FEAT))
    lens[a] = jnp.broadcast_to(len_in[...], (8, 128))

    barrier = pltpu.get_barrier_semaphore()
    greeted = [{"kvp": lax.rem(k + d, 16)} for d in range(1, 16)]
    greeted += [{"tp": mod4(t + d)} for d in range(1, 4)]
    greeted += [{"section": other}]
    greeted += [{"section": other, "tp": mod4(t + d)} for d in range(1, 4)]
    greeted += [{"section": other, **along_a(d)} for d in range(1, 4)]
    greeted += [{"section": other, **along_b(d)} for d in range(1, 4)]
    for dev in greeted:
        pl.semaphore_signal(barrier, inc=1, device_id=dev, device_id_type=pl.DeviceIdType.MESH)
    pl.semaphore_wait(barrier, len(greeted))

    def spread(l, h, src):
        spot = hid.at[l, rows(h * HALF + s * GROUP, GROUP), cols(t * HEAD, HEAD)]
        pending[l, h] = [send(src, spot, {"section": other})]
        for d in FAR_FIRST:
            pending[l, h] += [
                send(src, spot, {"tp": mod4(t + d)}),
                send(src, spot, {"tp": mod4(t + d), "section": other}),
            ]

    def front(l, h):
        for c in pending[l, h]:
            c.wait_recv()
        if h == 0:

            @pl.when(s != l)
            def _():
                pltpu.make_async_copy(gains.at[l], gains.at[l], wsem.at[l * 5 + 4]).wait()

        half = pl.ds(h * HALF, HALF)
        wide = hid[l, half, :].astype(F32)
        squares = wide * wide
        folded = (squares[:, 0:128] + squares[:, 128:256]) + (squares[:, 256:384] + squares[:, 384:512])
        squares_row = jnp.broadcast_to(jnp.sum(folded.T, axis=0, keepdims=True), (8, HALF))
        scaled[h] = (wide * gains[l, 0:1, :]).astype(BF)
        if h == 0:
            weight_wait(l, 0)
        for d in FAR_FIRST + (0,):
            pq[l, h, d, 0:HALF, :] = dot(scaled[h], wq[l, :, cols(mod4(a + d) * PAIR, PAIR)])
            pq[l, h, d, HALF:, :] = squares_row
            if d:
                first[l, h, d] = send(pq.at[l, h, d], rq.at[l, h, d - 1], along_a(d))
        if h == 0:
            weight_wait(l, 1)
            weight_wait(l, 2)
        pkv[l, h] = dot(scaled[h], wkv[l])
        for d in FAR_FIRST:
            piece = pkv.at[l, h, rows(mod4(a + d) * PIECE, PIECE), :]
            first_kv[l, h, d] = send(piece, rkv.at[l, h, d - 1], along_a(d))

    def sum_a(l, h):
        for d in FAR_FIRST:
            first[l, h, d].wait_recv()

        def summed(span):
            return (pq[l, h, 0, span, :] + rq[l, h, 0, span, :]) + (
                rq[l, h, 1, span, :] + rq[l, h, 2, span, :]
            )

        squares = summed(pl.ds(HALF, 8))
        for g in FAR_FIRST + (0,):
            c2[l, h, g, 0:PIECE, :] = summed(rows(mod4(b + g) * PIECE, PIECE))
            c2[l, h, g, PIECE:, :] = squares
            if g:
                second[l, h, g] = send(c2.at[l, h, g], r2.at[l, h, g - 1], along_b(g))

    def kv_a(l, h):
        for d in FAR_FIRST:
            first_kv[l, h, d].wait_recv()
        c2kv[l, h] = (pkv[l, h, rows(a * PIECE, PIECE), :] + rkv[l, h, 0]) + (rkv[l, h, 1] + rkv[l, h, 2])
        for d in FAR_FIRST:
            piece = c2kv.at[l, h, rows(mod4(b + d) * 16, 16), :]
            second_kv[l, h, d] = send(piece, r2kv.at[l, h, d - 1], along_b(d))

    def sum_b(l, h):
        for g in FAR_FIRST:
            second[l, h, g].wait_recv()
        full = (c2[l, h, 0] + r2[l, h, 0]) + (r2[l, h, 1] + r2[l, h, 2])
        factor = lax.rsqrt(full[PIECE : PIECE + 1] / D + 1e-05)
        fac[h] = jnp.broadcast_to(factor, (128, HALF)).T
        own_fac = fac[h, rows(b * PIECE, PIECE), :]
        own = rows(h * HALF + b * PIECE, PIECE)
        qry[l, own, :] = (full[0:PIECE] * jnp.concatenate([own_fac, own_fac], axis=1)).astype(BF)
        for d in FAR_FIRST:
            q_moves[l, h, d] = send(qry.at[l, own, :], qry.at[l, own, :], along_b(d))

    def kv_b(l, h):
        for d in FAR_FIRST:
            second_kv[l, h, d].wait_recv()
        kv_sum = (c2kv[l, h, rows(b * 16, 16), :] + r2kv[l, h, 0]) + (r2kv[l, h, 1] + r2kv[l, h, 2])
        kv_fac = fac[h, rows(a * PIECE + b * 16, 16), :]
        kv_rows = rows(h * HALF + a * PIECE + b * 16, 16)
        newkv[l, kv_rows, :] = (kv_sum * jnp.concatenate([kv_fac, kv_fac], axis=1)).astype(BF)
        kv_at[l, h] = used[0]
        used[0] += 16
        copies = kv_copies(l, h)
        for c in copies[1:]:
            c.start()

        @pl.when(b != 0)
        def _():
            copies[0].start()

    def kv_copies(l, h):
        spot = newkv.at[l, rows(h * HALF + a * PIECE + b * 16, 16), :]
        return [
            pltpu.make_async_remote_copy(
                src_ref=spot, dst_ref=spot, send_sem=ssem.at[kv_at[l, h] + d],
                recv_sem=rsem.at[kv_at[l, h] + d * 4 + b], device_id={"kvp": chip(mod4(a + d), 0)},
                device_id_type=pl.DeviceIdType.MESH,
            )
            for d in range(4)
        ]

    def kv_wait(l, h):
        for d in range(4):
            for j in range(4):
                if d or j:
                    dst = newkv.at[l, rows(h * HALF + mod4(a + 4 - d) * PIECE + j * 16, 16), :]
                    pltpu.make_async_copy(dst, dst, rsem.at[kv_at[l, h] + d * 4 + j]).wait()

    def attend(l, h):
        if h == 0:
            for d in range(4):
                cache_wait(l, d)
            if l == 0:
                for c in len_moves:
                    c.wait_recv()
        for d in FAR_FIRST:
            q_moves[l, h, d].wait_recv()

        def run(joint):
            parts = []
            for d in range(4):
                span = rows(h * HALF + mod4(b + 4 - d) * PIECE, PIECE)
                parts += [qry[l, span, 0:HEAD], qry[l, span, HEAD:PAIR]]
            q2 = jnp.concatenate(parts, axis=0)
            tops, sums, sides = [], [], []
            for c in (1, 2, 3, 0):
                if joint and c == 0:
                    kv_wait(l, h)
                place = pl.ds(c * SLOTS, SLOTS)
                bias = jnp.where(slot < lens[c, 0:1, 0:1], 0.0, -jnp.inf)
                scores = [dot_t(q2, kvc[l, 0, place, :]) + bias]
                values = [kvc[l, 1, place, :]]
                if joint and c == 0:
                    keys = (h + 1) * HALF
                    row_at = lax.rem(lax.broadcasted_iota(jnp.int32, (GROUP, keys), 0), PIECE)
                    key_at = lax.broadcasted_iota(jnp.int32, (GROUP, keys), 1)
                    ahead = key_at - row_at
                    causal = jnp.concatenate(
                        [
                            jnp.where(ahead <= h * HALF + (-d % 4) * PIECE, 0.0, -jnp.inf)
                            for d in range(4)
                        ],
                        axis=0,
                    )
                    scores.append(dot_t(q2, newkv[l, 0:keys, 0:HEAD]) + causal)
                    values.append(newkv[l, 0:keys, HEAD:PAIR])
                top = functools.reduce(
                    jnp.maximum, [jnp.max(v, axis=1, keepdims=True) for v in scores]
                )
                weights = [jnp.exp2((v - top) * EXP_SCALE) for v in scores]
                tops.append(top)
                sums.append(sum(jnp.sum(v, axis=1, keepdims=True) for v in weights))
                sides.append(sum(dot(w.astype(BF), v) for w, v in zip(weights, values)))
            peak = functools.reduce(jnp.maximum, tops)
            scale_by = [jnp.exp2((v - peak) * EXP_SCALE) for v in tops]
            total = sum(e * v for e, v in zip(scale_by, sums))
            merged = sum(e * v for e, v in zip(scale_by, sides))
            for d in range(4):
                piece = slice(d * GROUP, (d + 1) * GROUP)
                acc[l, h, d, 0:GROUP, :] = merged[piece]
                acc[l, h, d, GROUP:, :] = jnp.where(lane == 0, peak[piece], total[piece]).T[0:8]

        @pl.when(b == 0)
        def _():
            run(True)

        @pl.when(b != 0)
        def _():
            run(False)

        for d in (2, 3, 1):
            back[l, h, d] = send(acc.at[l, h, d], racc.at[l, h, d - 1], along_b(4 - d))

    def combine(l, h):
        for d in FAR_FIRST:
            back[l, h, d].wait_recv()
        own = rows(h * HALF + b * PIECE, PIECE)
        blocks = [acc[l, h, 0]] + [racc[l, h, d] for d in range(3)]
        stats = [jnp.concatenate([v[GROUP:]] * 16, axis=0).T for v in blocks]
        peaks = [v[:, 0:1] for v in stats]
        top = functools.reduce(jnp.maximum, peaks)
        scale_by = [jnp.exp2((v - top) * EXP_SCALE) for v in peaks]
        weight_sum = sum(e * v[:, 1:2] for e, v in zip(scale_by, stats))
        merged = sum(e * v[0:GROUP] for e, v in zip(scale_by, blocks))
        attended = (merged / weight_sum).astype(BF)
        att[l, a, own, 0:HEAD] = attended[0:PIECE]
        att[l, a, own, HEAD:PAIR] = attended[PIECE:GROUP]
        spot = att.at[l, a, own, :]
        for d in FAR_FIRST:
            near[l, h, d] = send(spot, spot, along_b(d))
        for e in FAR_FIRST:
            far[l, h, 0, e] = send(spot, spot, along_a(e))

    def forward(l, h):
        for d in (1, 3, 2):
            near[l, h, d].wait_recv()
            got = att.at[l, a, rows(h * HALF + mod4(b + 4 - d) * PIECE, PIECE), :]
            for e in FAR_FIRST:
                far[l, h, d, e] = send(got, got, along_a(e))

    def project(l, h):
        half = pl.ds(h * HALF, HALF)
        if h == 0:
            weight_wait(l, 3)
        summed = dot(att[l, a, half, :], wo[l, rows(a * PAIR, PAIR), :])
        for e in (1, 3, 2):
            for d in (0, 1, 3, 2):
                far[l, h, d, e].wait_recv()
            source = mod4(a + 4 - e)
            summed += dot(att[l, source, half, :], wo[l, rows(source * PAIR, PAIR), :])
        mix[l, half, :] = summed
        swaps[l, h] = send(
            mix.at[l, rows(h * HALF + other * GROUP, GROUP), :], rmix.at[l, h], {"section": other}
        )

    def turn(l, h):
        swaps[l, h].wait_recv()
        kept = rows(h * HALF + s * GROUP, GROUP)
        for d in FAR_FIRST + (0,):
            block = cols(mod4(t + d) * HEAD, HEAD)
            zs[l, h, d] = mix[l, kept, block] + rmix[l, h, :, block]
            if d:
                turns[l, h, d] = send(zs.at[l, h, d], zr.at[l, h, d - 1], {"tp": mod4(t + d)})

    def settle(l, h):
        for d in FAR_FIRST:
            turns[l, h, d].wait_recv()
        kept = rows(h * HALF + s * GROUP, GROUP)
        mine_cols = cols(t * HEAD, HEAD)
        update = (zs[l, h, 0] + zr[l, h, 0]) + (zr[l, h, 1] + zr[l, h, 2])
        after = (hid[l, kept, mine_cols].astype(F32) + update).astype(BF)
        fin[l, kept, :] = after
        if l + 1 < LAYERS:
            hid[l + 1, kept, mine_cols] = after
            spread(l + 1, h, fin.at[l, kept, :])
        else:
            ends.append(send(fin.at[l, kept, :], fin.at[l, kept, :], {"section": other}))

    pending, first, first_kv, second, second_kv = {}, {}, {}, {}, {}
    q_moves, kv_at, back, near, far, swaps, turns = {}, {}, {}, {}, {}, {}, {}
    ends = []
    lane = lax.rem(lax.broadcasted_iota(jnp.int32, (GROUP, 128), 1), 2)
    slot = lax.broadcasted_iota(jnp.int32, (1, SLOTS), 1)

    for h in range(2):
        spread(0, h, tok.at[rows(h * HALF + s * GROUP, GROUP), :])
    remote_w = weights_remote()
    for i in (0, 4, 1, 2, 3):
        remote_w[i].start()
    remote_k, remote_v = cache_remote(0), cache_remote(1)
    remote_c = remote_k + remote_v

    @pl.when(s == 0)
    def _():
        for c in remote_k:
            c.start()

    len_moves = [send(lens.at[a], lens.at[a], along_a(d)) for d in FAR_FIRST]
    for h in range(2):
        kept = rows(h * HALF + s * GROUP, GROUP)
        hid[0, kept, cols(t * HEAD, HEAD)] = tok[kept, :]
    drained = [0]

    def drain(upto):
        for c in started[drained[0] : upto]:
            c.wait_send()
        drained[0] = max(drained[0], upto)

    steps = (front, sum_a, kv_a, sum_b, kv_b, attend, combine, forward, project, turn, settle)
    order = sorted(
        (PERIOD * (i // len(steps)) + STARTS[i % len(steps)] + LAG * h, h, i)
        for h in range(2)
        for i in range(LAYERS * len(steps))
    )
    marks = {}
    for _, h, i in order:
        l, step = i // len(steps), steps[i % len(steps)]
        if step == sum_b and h == 0 and l > 0:
            drain(marks[0])
        if step == sum_a and h == 0:
            marks[l] = len(started)
        if step == turn and l == 0 and h == 0:

            @pl.when(s == 1)
            def _():
                for c in remote_c:
                    c.start()

        step(l, h)
        if step == front and l == 0 and h == 0:

            @pl.when(s == 0)
            def _():
                for c in remote_v:
                    c.start()

    for c in ends:
        c.wait_recv()
    out[...] = jnp.where(s == 0, hid[1, :, cols(t * HEAD, HEAD)], fin[1])
    drain(len(started))
    for c in remote_w + remote_c:
        c.wait_send()

    moved = [kv_copies(l, h) for l in range(LAYERS) for h in range(2)]
    for copies in moved:
        for c in copies[1:]:
            c.wait_send()

    @pl.when(b != 0)
    def _():
        for copies in moved:
            copies[0].wait_send()


def per_device(tokens, norm_gain, query_weight, kv_weight, out_weight, cache, lengths):
    vmem = pl.BlockSpec(memory_space=pltpu.VMEM)
    anywhere = pl.BlockSpec(memory_space=pl.ANY)
    n = 300
    dma = pltpu.SemaphoreType.DMA
    scratch = [
        pltpu.VMEM((2, FEAT, 1024), BF),
        pltpu.VMEM((2, FEAT, PAIR), BF),
        pltpu.VMEM((2, 1024, FEAT), BF),
        pltpu.VMEM((2, 2, 4 * SLOTS, HEAD), BF),
        pltpu.VMEM((2, ROWS, FEAT), BF),
        pltpu.VMEM((2, HALF, FEAT), BF),
        pltpu.VMEM((2, 8, FEAT), F32),
        pltpu.VMEM((4, 8, 128), jnp.int32),
        pltpu.VMEM((2, 2, 4, HALF + 8, PAIR), F32),
        pltpu.VMEM((2, 2, 3, HALF + 8, PAIR), F32),
        pltpu.VMEM((2, 2, HALF, PAIR), F32),
        pltpu.VMEM((2, 2, 3, PIECE, PAIR), F32),
        pltpu.VMEM((2, HALF, 128), F32),
        pltpu.VMEM((2, 2, 4, PIECE + 8, PAIR), F32),
        pltpu.VMEM((2, 2, 3, PIECE + 8, PAIR), F32),
        pltpu.VMEM((2, 2, PIECE, PAIR), F32),
        pltpu.VMEM((2, 2, 3, 16, PAIR), F32),
        pltpu.VMEM((2, ROWS, PAIR), BF),
        pltpu.VMEM((2, ROWS, PAIR), BF),
        pltpu.VMEM((2, 2, 4, GROUP + 8, 128), F32),
        pltpu.VMEM((2, 2, 3, GROUP + 8, 128), F32),
        pltpu.VMEM((2, 4, ROWS, PAIR), BF),
        pltpu.VMEM((2, ROWS, FEAT), F32),
        pltpu.VMEM((2, 2, GROUP, FEAT), F32),
        pltpu.VMEM((2, 2, 4, GROUP, HEAD), F32),
        pltpu.VMEM((2, 2, 3, GROUP, HEAD), F32),
        pltpu.VMEM((2, ROWS, HEAD), BF),
        dma((n,)), dma((n,)), dma((10,)), dma((5,)), dma((16,)), dma((14,)),
    ]
    result = pl.pallas_call(
        kernel,
        out_shape=jax.ShapeDtypeStruct((ROWS, HEAD), BF),
        in_specs=[vmem, vmem, anywhere, anywhere, anywhere, anywhere, vmem],
        out_specs=vmem,
        scratch_shapes=scratch,
        compiler_params=pltpu.CompilerParams(
            collective_id=0, has_side_effects=True, vmem_limit_bytes=60 * 2**20
        ),
    )(tokens, norm_gain, query_weight, kv_weight, out_weight, cache, lengths[None])
    return result[None]


def solution(mesh):
    placed = (
        P(None, ("kvp", "tp")),
        P("section", "kvp"),
        P("section", "kvp", "tp"),
        P("section", None, "kvp", "tp"),
        P("section", "tp", "kvp"),
        P("section", None, "kvp", "tp"),
        P("kvp"),
    )
    return jax.shard_map(
        per_device,
        mesh=mesh,
        in_specs=placed,
        out_specs=P("section", None, ("kvp", "tp")),
        check_vma=False,
    )
```

```python
import functools
import math

import jax
import jax.numpy as jnp
from jax import lax
from jax.experimental import pallas as pl
from jax.experimental.pallas import tpu as pltpu
from jax.sharding import PartitionSpec as P

LAYERS = 2
ROWS = 512
HALF = 256
GROUP = 128
PIECE = 64
D = 8192
FEAT = 512
HEAD = 128
PAIR = 256
SLOTS = 1024
EXP_SCALE = math.log2(math.e) / math.sqrt(HEAD)
BF = jnp.bfloat16
F32 = jnp.float32
FAR_FIRST = (2, 1, 3)
STARTS = (0, 1, 1.1, 2, 2.1, 3, 4, 5, 6, 7, 8)
PERIOD = 9
LAG = 1.5


def mod4(value):
    return lax.rem(value, 4)


def dot(left, right):
    return jnp.dot(left, right, preferred_element_type=F32)


def dot_t(left, right):
    return lax.dot_general(left, right, (((1,), (1,)), ((), ())), preferred_element_type=F32)


def kernel(
    tok, gain, wq_in, wkv_in, wo_in, cache_in, len_in, out,
    wq, wkv, wo, kvc, hid, scaled, gains, lens, pq, rq, pkv, rkv, fac,
    c2, r2, c2kv, r2kv, qry, newkv, acc, racc, att,
    mix, rmix, zs, zr, fin, ssem, rsem, wsem, wssem, csem, cssem,
):
    s = lax.axis_index("section")
    k = lax.axis_index("kvp")
    t = lax.axis_index("tp")
    y = k // 4
    x = lax.rem(k, 4)
    a = (1 - s) * x + s * y
    b = (1 - s) * y + s * x
    other = 1 - s

    def chip(i, j):
        return i * (1 + 3 * s) + j * (4 - 3 * s)

    def along_a(d):
        return {"kvp": chip(mod4(a + d), b)}

    def along_b(d):
        return {"kvp": chip(a, mod4(b + d))}

    def rows(start, size):
        return pl.ds(pl.multiple_of(start, 16), size)

    def cols(start, size):
        return pl.ds(pl.multiple_of(start, 128), size)

    used = [0]
    started = []

    def send(src, dst, dev):
        i = used[0]
        used[0] += 1
        c = pltpu.make_async_remote_copy(
            src_ref=src, dst_ref=dst, send_sem=ssem.at[i], recv_sem=rsem.at[i],
            device_id=dev, device_id_type=pl.DeviceIdType.MESH,
        )
        c.start()
        started.append(c)
        return c

    def weight_parts(h):
        return [
            (wq_in.at[0, :, cols(h * 1024, 1024)], wq.at[s]),
            (wkv_in.at[0, 0, :, cols(h * HEAD, HEAD)], wkv.at[s, :, pl.ds(0, HEAD)]),
            (wkv_in.at[0, 1, :, cols(h * HEAD, HEAD)], wkv.at[s, :, pl.ds(HEAD, HEAD)]),
            (wo_in.at[0, rows(h * 1024, 1024), :], wo.at[s]),
        ]

    def weights_local():
        return [
            pltpu.make_async_copy(src, dst, wsem.at[s * 5 + i])
            for i, (src, dst) in enumerate(weight_parts(s))
        ]

    def weights_remote():
        parts = weight_parts(other) + [(gains.at[s], gains.at[s])]
        return [
            pltpu.make_async_remote_copy(
                src_ref=src, dst_ref=dst, send_sem=wssem.at[i], recv_sem=wsem.at[s * 5 + i],
                device_id={"section": other}, device_id_type=pl.DeviceIdType.MESH,
            )
            for i, (src, dst) in enumerate(parts)
        ]

    def weight_wait(l, i):
        dst = (wq.at[l], wkv.at[l, :, pl.ds(0, HEAD)], wkv.at[l, :, pl.ds(HEAD, HEAD)], wo.at[l])[i]
        pltpu.make_async_copy(dst, dst, wsem.at[l * 5 + i]).wait()

    def cache_local():
        return [
            pltpu.make_async_copy(
                cache_in.at[0, i, :, cols(s * HEAD, HEAD)],
                kvc.at[s, i, rows(a * SLOTS, SLOTS), :],
                csem.at[s * 8 + i],
            )
            for i in range(2)
        ]

    def cache_remote(i):
        made = []

        def add(head, place, d, dev):
            made.append(
                pltpu.make_async_remote_copy(
                    src_ref=cache_in.at[0, i, :, cols(head * HEAD, HEAD)],
                    dst_ref=kvc.at[s, i, rows(place * SLOTS, SLOTS), :],
                    send_sem=cssem.at[i * 7 + len(made)], recv_sem=csem.at[s * 8 + d * 2 + i],
                    device_id=dev, device_id_type=pl.DeviceIdType.MESH,
                )
            )

        add(other, b, 0, {"section": other})
        for d in FAR_FIRST:
            add(s, a, d, along_a(d))
            add(other, b, d, {"section": other, **along_b(d)})
        return made

    def cache_wait(l, d):
        for i in range(2):
            dst = kvc.at[l, i, rows(mod4(a + 4 - d) * SLOTS, SLOTS), :]
            pltpu.make_async_copy(dst, dst, csem.at[l * 8 + d * 2 + i]).wait()

    local = weights_local()
    for c in local:
        c.start()
    for c in cache_local():
        c.start()
    gains[s] = jnp.broadcast_to(gain[...].astype(F32), (8, FEAT))
    lens[a] = jnp.broadcast_to(len_in[...], (8, 128))

    barrier = pltpu.get_barrier_semaphore()
    greeted = [{"kvp": lax.rem(k + d, 16)} for d in range(1, 16)]
    greeted += [{"tp": mod4(t + d)} for d in range(1, 4)]
    greeted += [{"section": other}]
    greeted += [{"section": other, "tp": mod4(t + d)} for d in range(1, 4)]
    greeted += [{"section": other, **along_a(d)} for d in range(1, 4)]
    greeted += [{"section": other, **along_b(d)} for d in range(1, 4)]
    for dev in greeted:
        pl.semaphore_signal(barrier, inc=1, device_id=dev, device_id_type=pl.DeviceIdType.MESH)
    pl.semaphore_wait(barrier, len(greeted))

    def spread(l, h, src):
        spot = hid.at[l, rows(h * HALF + s * GROUP, GROUP), cols(t * HEAD, HEAD)]
        pending[l, h] = [send(src, spot, {"section": other})]
        for d in FAR_FIRST:
            pending[l, h] += [
                send(src, spot, {"tp": mod4(t + d)}),
                send(src, spot, {"tp": mod4(t + d), "section": other}),
            ]

    def front(l, h):
        for c in pending[l, h]:
            c.wait_recv()
        if h == 0:

            @pl.when(s != l)
            def _():
                pltpu.make_async_copy(gains.at[l], gains.at[l], wsem.at[l * 5 + 4]).wait()

        half = pl.ds(h * HALF, HALF)
        wide = hid[l, half, :].astype(F32)
        squares = wide * wide
        folded = (squares[:, 0:128] + squares[:, 128:256]) + (squares[:, 256:384] + squares[:, 384:512])
        squares_row = jnp.broadcast_to(jnp.sum(folded.T, axis=0, keepdims=True), (8, HALF))
        scaled[h] = (wide * gains[l, 0:1, :]).astype(BF)
        if h == 0:
            weight_wait(l, 0)
        for d in FAR_FIRST + (0,):
            pq[l, h, d, 0:HALF, :] = dot(scaled[h], wq[l, :, cols(mod4(a + d) * PAIR, PAIR)])
            pq[l, h, d, HALF:, :] = squares_row
            if d:
                first[l, h, d] = send(pq.at[l, h, d], rq.at[l, h, d - 1], along_a(d))
        if h == 0:
            weight_wait(l, 1)
            weight_wait(l, 2)
        pkv[l, h] = dot(scaled[h], wkv[l])
        for d in FAR_FIRST:
            piece = pkv.at[l, h, rows(mod4(a + d) * PIECE, PIECE), :]
            first_kv[l, h, d] = send(piece, rkv.at[l, h, d - 1], along_a(d))

    def sum_a(l, h):
        for d in FAR_FIRST:
            first[l, h, d].wait_recv()

        def summed(span):
            return (pq[l, h, 0, span, :] + rq[l, h, 0, span, :]) + (
                rq[l, h, 1, span, :] + rq[l, h, 2, span, :]
            )

        squares = summed(pl.ds(HALF, 8))
        for g in FAR_FIRST + (0,):
            c2[l, h, g, 0:PIECE, :] = summed(rows(mod4(b + g) * PIECE, PIECE))
            c2[l, h, g, PIECE:, :] = squares
            if g:
                second[l, h, g] = send(c2.at[l, h, g], r2.at[l, h, g - 1], along_b(g))

    def kv_a(l, h):
        for d in FAR_FIRST:
            first_kv[l, h, d].wait_recv()
        c2kv[l, h] = (pkv[l, h, rows(a * PIECE, PIECE), :] + rkv[l, h, 0]) + (rkv[l, h, 1] + rkv[l, h, 2])
        for d in FAR_FIRST:
            piece = c2kv.at[l, h, rows(mod4(b + d) * 16, 16), :]
            second_kv[l, h, d] = send(piece, r2kv.at[l, h, d - 1], along_b(d))

    def sum_b(l, h):
        for g in FAR_FIRST:
            second[l, h, g].wait_recv()
        full = (c2[l, h, 0] + r2[l, h, 0]) + (r2[l, h, 1] + r2[l, h, 2])
        factor = lax.rsqrt(full[PIECE : PIECE + 1] / D + 1e-05)
        fac[h] = jnp.broadcast_to(factor, (128, HALF)).T
        own_fac = fac[h, rows(b * PIECE, PIECE), :]
        own = rows(h * HALF + b * PIECE, PIECE)
        qry[l, own, :] = (full[0:PIECE] * jnp.concatenate([own_fac, own_fac], axis=1)).astype(BF)
        for d in FAR_FIRST:
            q_moves[l, h, d] = send(qry.at[l, own, :], qry.at[l, own, :], along_b(d))

    def kv_b(l, h):
        for d in FAR_FIRST:
            second_kv[l, h, d].wait_recv()
        kv_sum = (c2kv[l, h, rows(b * 16, 16), :] + r2kv[l, h, 0]) + (r2kv[l, h, 1] + r2kv[l, h, 2])
        kv_fac = fac[h, rows(a * PIECE + b * 16, 16), :]
        kv_rows = rows(h * HALF + a * PIECE + b * 16, 16)
        newkv[l, kv_rows, :] = (kv_sum * jnp.concatenate([kv_fac, kv_fac], axis=1)).astype(BF)
        kv_at[l, h] = used[0]
        used[0] += 16
        copies = kv_copies(l, h)
        for c in copies[1:]:
            c.start()

        @pl.when(b != 0)
        def _():
            copies[0].start()

    def kv_copies(l, h):
        spot = newkv.at[l, rows(h * HALF + a * PIECE + b * 16, 16), :]
        return [
            pltpu.make_async_remote_copy(
                src_ref=spot, dst_ref=spot, send_sem=ssem.at[kv_at[l, h] + d],
                recv_sem=rsem.at[kv_at[l, h] + d * 4 + b], device_id={"kvp": chip(mod4(a + d), 0)},
                device_id_type=pl.DeviceIdType.MESH,
            )
            for d in range(4)
        ]

    def kv_wait(l, h):
        for d in range(4):
            for j in range(4):
                if d or j:
                    dst = newkv.at[l, rows(h * HALF + mod4(a + 4 - d) * PIECE + j * 16, 16), :]
                    pltpu.make_async_copy(dst, dst, rsem.at[kv_at[l, h] + d * 4 + j]).wait()

    def attend(l, h):
        if h == 0:
            for d in range(4):
                cache_wait(l, d)
            if l == 0:
                for c in len_moves:
                    c.wait_recv()
        for d in FAR_FIRST:
            q_moves[l, h, d].wait_recv()

        def run(joint):
            parts = []
            for d in range(4):
                span = rows(h * HALF + mod4(b + 4 - d) * PIECE, PIECE)
                parts += [qry[l, span, 0:HEAD], qry[l, span, HEAD:PAIR]]
            q2 = jnp.concatenate(parts, axis=0)
            tops, sums, sides = [], [], []
            for c in (1, 2, 3, 0):
                if joint and c == 0:
                    kv_wait(l, h)
                place = pl.ds(c * SLOTS, SLOTS)
                bias = jnp.where(slot < lens[c, 0:1, 0:1], 0.0, -jnp.inf)
                scores = [dot_t(q2, kvc[l, 0, place, :]) + bias]
                values = [kvc[l, 1, place, :]]
                if joint and c == 0:
                    keys = (h + 1) * HALF
                    row_at = lax.rem(lax.broadcasted_iota(jnp.int32, (GROUP, keys), 0), PIECE)
                    key_at = lax.broadcasted_iota(jnp.int32, (GROUP, keys), 1)
                    ahead = key_at - row_at
                    causal = jnp.concatenate(
                        [
                            jnp.where(ahead <= h * HALF + (-d % 4) * PIECE, 0.0, -jnp.inf)
                            for d in range(4)
                        ],
                        axis=0,
                    )
                    scores.append(dot_t(q2, newkv[l, 0:keys, 0:HEAD]) + causal)
                    values.append(newkv[l, 0:keys, HEAD:PAIR])
                top = functools.reduce(
                    jnp.maximum, [jnp.max(v, axis=1, keepdims=True) for v in scores]
                )
                weights = [jnp.exp2((v - top) * EXP_SCALE) for v in scores]
                tops.append(top)
                sums.append(sum(jnp.sum(v, axis=1, keepdims=True) for v in weights))
                sides.append(sum(dot(w.astype(BF), v) for w, v in zip(weights, values)))
            peak = functools.reduce(jnp.maximum, tops)
            scale_by = [jnp.exp2((v - peak) * EXP_SCALE) for v in tops]
            total = sum(e * v for e, v in zip(scale_by, sums))
            merged = sum(e * v for e, v in zip(scale_by, sides))
            for d in range(4):
                piece = slice(d * GROUP, (d + 1) * GROUP)
                acc[l, h, d, 0:GROUP, :] = merged[piece]
                acc[l, h, d, GROUP:, :] = jnp.where(lane == 0, peak[piece], total[piece]).T[0:8]

        @pl.when(b == 0)
        def _():
            run(True)

        @pl.when(b != 0)
        def _():
            run(False)

        for d in (2, 3, 1):
            back[l, h, d] = send(acc.at[l, h, d], racc.at[l, h, d - 1], along_b(4 - d))

    def combine(l, h):
        for d in FAR_FIRST:
            back[l, h, d].wait_recv()
        own = rows(h * HALF + b * PIECE, PIECE)
        blocks = [acc[l, h, 0]] + [racc[l, h, d] for d in range(3)]
        stats = [jnp.concatenate([v[GROUP:]] * 16, axis=0).T for v in blocks]
        peaks = [v[:, 0:1] for v in stats]
        top = functools.reduce(jnp.maximum, peaks)
        scale_by = [jnp.exp2((v - top) * EXP_SCALE) for v in peaks]
        weight_sum = sum(e * v[:, 1:2] for e, v in zip(scale_by, stats))
        merged = sum(e * v[0:GROUP] for e, v in zip(scale_by, blocks))
        attended = (merged / weight_sum).astype(BF)
        att[l, a, own, 0:HEAD] = attended[0:PIECE]
        att[l, a, own, HEAD:PAIR] = attended[PIECE:GROUP]
        spot = att.at[l, a, own, :]
        for d in FAR_FIRST:
            near[l, h, d] = send(spot, spot, along_b(d))
        for e in FAR_FIRST:
            far[l, h, 0, e] = send(spot, spot, along_a(e))

    def forward(l, h):
        for d in (1, 3, 2):
            near[l, h, d].wait_recv()
            got = att.at[l, a, rows(h * HALF + mod4(b + 4 - d) * PIECE, PIECE), :]
            for e in FAR_FIRST:
                far[l, h, d, e] = send(got, got, along_a(e))

    def project(l, h):
        half = pl.ds(h * HALF, HALF)
        if h == 0:
            weight_wait(l, 3)
        summed = dot(att[l, a, half, :], wo[l, rows(a * PAIR, PAIR), :])
        for e in (1, 3, 2):
            for d in (0, 1, 3, 2):
                far[l, h, d, e].wait_recv()
            source = mod4(a + 4 - e)
            summed += dot(att[l, source, half, :], wo[l, rows(source * PAIR, PAIR), :])
        mix[l, half, :] = summed
        swaps[l, h] = send(
            mix.at[l, rows(h * HALF + other * GROUP, GROUP), :], rmix.at[l, h], {"section": other}
        )

    def turn(l, h):
        swaps[l, h].wait_recv()
        kept = rows(h * HALF + s * GROUP, GROUP)
        for d in FAR_FIRST + (0,):
            block = cols(mod4(t + d) * HEAD, HEAD)
            zs[l, h, d] = mix[l, kept, block] + rmix[l, h, :, block]
            if d:
                turns[l, h, d] = send(zs.at[l, h, d], zr.at[l, h, d - 1], {"tp": mod4(t + d)})

    def settle(l, h):
        for d in FAR_FIRST:
            turns[l, h, d].wait_recv()
        kept = rows(h * HALF + s * GROUP, GROUP)
        mine_cols = cols(t * HEAD, HEAD)
        update = (zs[l, h, 0] + zr[l, h, 0]) + (zr[l, h, 1] + zr[l, h, 2])
        after = (hid[l, kept, mine_cols].astype(F32) + update).astype(BF)
        fin[l, kept, :] = after
        if l + 1 < LAYERS:
            hid[l + 1, kept, mine_cols] = after
            spread(l + 1, h, fin.at[l, kept, :])
        else:
            ends.append(send(fin.at[l, kept, :], fin.at[l, kept, :], {"section": other}))

    pending, first, first_kv, second, second_kv = {}, {}, {}, {}, {}
    q_moves, kv_at, back, near, far, swaps, turns = {}, {}, {}, {}, {}, {}, {}
    ends = []
    lane = lax.rem(lax.broadcasted_iota(jnp.int32, (GROUP, 128), 1), 2)
    slot = lax.broadcasted_iota(jnp.int32, (1, SLOTS), 1)

    for h in range(2):
        spread(0, h, tok.at[rows(h * HALF + s * GROUP, GROUP), :])
    remote_w = weights_remote()
    for i in (0, 4, 1, 2, 3):
        remote_w[i].start()
    remote_k, remote_v = cache_remote(0), cache_remote(1)
    remote_c = remote_k + remote_v

    @pl.when(s == 0)
    def _():
        for c in remote_k:
            c.start()

    len_moves = [send(lens.at[a], lens.at[a], along_a(d)) for d in FAR_FIRST]
    for h in range(2):
        kept = rows(h * HALF + s * GROUP, GROUP)
        hid[0, kept, cols(t * HEAD, HEAD)] = tok[kept, :]
    drained = [0]

    def drain(upto):
        for c in started[drained[0] : upto]:
            c.wait_send()
        drained[0] = max(drained[0], upto)

    steps = (front, sum_a, kv_a, sum_b, kv_b, attend, combine, forward, project, turn, settle)
    order = sorted(
        (PERIOD * (i // len(steps)) + STARTS[i % len(steps)] + LAG * h, h, i)
        for h in range(2)
        for i in range(LAYERS * len(steps))
    )
    marks = {}
    for _, h, i in order:
        l, step = i // len(steps), steps[i % len(steps)]
        if step == sum_b and h == 0 and l > 0:
            drain(marks[0])
        if step == sum_a and h == 0:
            marks[l] = len(started)
        if step == turn and l > 0 and h == 0:
            drain(marks[l])
        if step == turn and l == 0 and h == 0:

            @pl.when(s == 1)
            def _():
                for c in remote_c:
                    c.start()

        step(l, h)
        if step == sum_a and l == 0 and h == 0:

            @pl.when(s == 0)
            def _():
                for c in remote_v:
                    c.start()

    for c in ends:
        c.wait_recv()
    out[...] = jnp.where(s == 0, hid[1, :, cols(t * HEAD, HEAD)], fin[1])
    drain(len(started))
    for c in remote_w + remote_c:
        c.wait_send()

    moved = [kv_copies(l, h) for l in range(LAYERS) for h in range(2)]
    for copies in moved:
        for c in copies[1:]:
            c.wait_send()

    @pl.when(b != 0)
    def _():
        for copies in moved:
            copies[0].wait_send()


def per_device(tokens, norm_gain, query_weight, kv_weight, out_weight, cache, lengths):
    vmem = pl.BlockSpec(memory_space=pltpu.VMEM)
    anywhere = pl.BlockSpec(memory_space=pl.ANY)
    n = 300
    dma = pltpu.SemaphoreType.DMA
    scratch = [
        pltpu.VMEM((2, FEAT, 1024), BF),
        pltpu.VMEM((2, FEAT, PAIR), BF),
        pltpu.VMEM((2, 1024, FEAT), BF),
        pltpu.VMEM((2, 2, 4 * SLOTS, HEAD), BF),
        pltpu.VMEM((2, ROWS, FEAT), BF),
        pltpu.VMEM((2, HALF, FEAT), BF),
        pltpu.VMEM((2, 8, FEAT), F32),
        pltpu.VMEM((4, 8, 128), jnp.int32),
        pltpu.VMEM((2, 2, 4, HALF + 8, PAIR), F32),
        pltpu.VMEM((2, 2, 3, HALF + 8, PAIR), F32),
        pltpu.VMEM((2, 2, HALF, PAIR), F32),
        pltpu.VMEM((2, 2, 3, PIECE, PAIR), F32),
        pltpu.VMEM((2, HALF, 128), F32),
        pltpu.VMEM((2, 2, 4, PIECE + 8, PAIR), F32),
        pltpu.VMEM((2, 2, 3, PIECE + 8, PAIR), F32),
        pltpu.VMEM((2, 2, PIECE, PAIR), F32),
        pltpu.VMEM((2, 2, 3, 16, PAIR), F32),
        pltpu.VMEM((2, ROWS, PAIR), BF),
        pltpu.VMEM((2, ROWS, PAIR), BF),
        pltpu.VMEM((2, 2, 4, GROUP + 8, 128), F32),
        pltpu.VMEM((2, 2, 3, GROUP + 8, 128), F32),
        pltpu.VMEM((2, 4, ROWS, PAIR), BF),
        pltpu.VMEM((2, ROWS, FEAT), F32),
        pltpu.VMEM((2, 2, GROUP, FEAT), F32),
        pltpu.VMEM((2, 2, 4, GROUP, HEAD), F32),
        pltpu.VMEM((2, 2, 3, GROUP, HEAD), F32),
        pltpu.VMEM((2, ROWS, HEAD), BF),
        dma((n,)), dma((n,)), dma((10,)), dma((5,)), dma((16,)), dma((14,)),
    ]
    result = pl.pallas_call(
        kernel,
        out_shape=jax.ShapeDtypeStruct((ROWS, HEAD), BF),
        in_specs=[vmem, vmem, anywhere, anywhere, anywhere, anywhere, vmem],
        out_specs=vmem,
        scratch_shapes=scratch,
        compiler_params=pltpu.CompilerParams(
            collective_id=0, has_side_effects=True, vmem_limit_bytes=60 * 2**20
        ),
    )(tokens, norm_gain, query_weight, kv_weight, out_weight, cache, lengths[None])
    return result[None]


def solution(mesh):
    placed = (
        P(None, ("kvp", "tp")),
        P("section", "kvp"),
        P("section", "kvp", "tp"),
        P("section", None, "kvp", "tp"),
        P("section", "tp", "kvp"),
        P("section", None, "kvp", "tp"),
        P("kvp"),
    )
    return jax.shard_map(
        per_device,
        mesh=mesh,
        in_specs=placed,
        out_specs=P("section", None, ("kvp", "tp")),
        check_vma=False,
    )
```
